32 devices in a mesh: bucket: 4 (over y, x), head: 8 (over z, core).
Axes of the slice: x: 2, y: 2, z: 4, core: 2. Of those that a mesh axis runs over, the one named last changes fastest.
Arguments:
- queries: bfloat16 [4096, 4096], P(('bucket', 'head')), may hold values from -25 to 25
- keys: bfloat16 [4096, 4096], P(('bucket', 'head')), may hold values from -6 to 6
- values: bfloat16 [4096, 4096], P(('bucket', 'head')), may hold values from -6 to 6
- grad_out: bfloat16 [4096, 4096], P(('bucket', 'head')), may hold values from -6 to 6
- page_dest: int32 [128], replicated, may hold values from 0 to 127, as said below
- doc_start: int32 [128], replicated, may hold values from 0 to 24, as said below
Outputs:
- grad_queries: bfloat16 [4096, 4096], P(('bucket', 'head'))
- grad_keys: bfloat16 [4096, 4096], P(('bucket', 'head'))
- grad_values: bfloat16 [4096, 4096], P(('bucket', 'head'))
The draws below stay inside these ranges and needn't reach their ends.
Inputs may be any that keep to these rules, and one draw needn't show every extreme that they name: Page p holds window tokens p * 32 to p * 32 + 31. page_dest[p] = bucket * 32 + slot; the 4 pages of each device go one to each bucket, and every slot of every bucket is named by exactly one page. doc_start[bucket * 32 + slot] is the first slot of the document that holds that slot. Documents are runs of slots of one bucket, of lengths that are multiples of 8 slots, from 8 to 32; some bucket holds one document and some bucket ends with a document of the least length.
All inputs are finite; a program needn't handle non-finite values.
Results may differ from the reference program's by a relative error of at most 0.0081.
Values may be sent and summed in bfloat16 or wider, within the bound.
A program may use at most 128 MiB of HBM per device.

```python
import jax
import jax.numpy as jnp
from jax import lax

HEADS = 32
HD = 128
PAGE = 32
SLOTS = 32
SEG = 1024
TOKENS = 4096
PAGES = 128
N_BUCKET = 4
N_HEAD = 8


def drawn_rows(key, salt):
    drawn = jax.random.normal(jax.random.fold_in(key, salt), (TOKENS, HEADS * HD), jnp.float32)
    return jnp.clip(drawn, -6.0, 6.0)


def draw_keys(key, part):
    drawn = drawn_rows(key, 2)
    return drawn.astype(jnp.bfloat16)


def draw_queries(key, part):
    drawn = drawn_rows(key, 1)
    return drawn.astype(jnp.bfloat16)


def device_perm(row_key):
    return jax.random.permutation(row_key, N_BUCKET).astype(jnp.int32)


def bucket_perm(row_key):
    return jax.random.permutation(row_key, SLOTS).astype(jnp.int32)


def draw_page_dest(key, part):
    row_keys = jax.random.split(jax.random.fold_in(key, 51), SLOTS)
    targets = jax.vmap(device_perm)(row_keys)
    slot_keys = jax.random.split(jax.random.fold_in(key, 52), N_BUCKET)
    slot_perm = jax.vmap(bucket_perm)(slot_keys)
    slots_taken = jnp.take_along_axis(jnp.transpose(slot_perm), targets, axis=1)
    return (targets * SLOTS + slots_taken).reshape(PAGES).astype(jnp.int32)


def draw_doc_start(key, part):
    units = N_HEAD // 2
    unit_len = 2 * N_BUCKET
    flags = jax.random.randint(jax.random.fold_in(key, 41), (N_BUCKET, units), 0, 2).astype(jnp.int32)
    whole = jax.random.randint(jax.random.fold_in(key, 42), (), 0, N_BUCKET).astype(jnp.int32)
    unit_range = jnp.arange(units, dtype=jnp.int32)
    bucket_range = jnp.arange(N_BUCKET, dtype=jnp.int32)
    flags = jnp.where(unit_range[None, :] == 0, 1, flags)
    flags = jnp.where((bucket_range[:, None] == whole) & (unit_range[None, :] > 0), 0, flags)
    flags = jnp.where((bucket_range[:, None] == (whole + 1) % N_BUCKET) & (unit_range[None, :] == units - 1), 1, flags)
    starts = lax.cummax(jnp.where(flags == 1, unit_range[None, :], 0), axis=1)
    slot_starts = jnp.repeat(starts * unit_len, unit_len, axis=1)
    return slot_starts.reshape(PAGES).astype(jnp.int32)


def block_scale(key, shape, pieces, low, high):
    level = 1.0
    for dim, shards_of in pieces:
        heights = jax.random.uniform(jax.random.fold_in(jax.random.fold_in(key, 6), dim), (shards_of,), jnp.float32, low / len(pieces), high / len(pieces))
        level = level * jnp.repeat(jnp.exp(heights), shape[dim] // shards_of).reshape((-1,) + (1,) * (len(shape) - 1 - dim))
    return level


def noise(rng, extent, deviation, limit, cuts=(), kind=jnp.bfloat16):
    values = deviation * jax.random.normal(rng, extent, jnp.float32)
    if cuts:
        values = values * block_scale(rng, extent, cuts, -0.22, 0.18)
    return jnp.clip(values, -limit, limit).astype(kind)


def setup_inputs(seed: int = 0) -> dict:
    arg_keys = jax.random.split(jax.random.key(seed), 7)
    queries = draw_queries(jax.random.fold_in(arg_keys[6], 71), 0)
    keys = draw_keys(jax.random.fold_in(arg_keys[6], 71), 0)
    values = noise(arg_keys[2], (TOKENS, HEADS * HD), 1.0, 6.0, ((0, 32),))
    grad_out = noise(arg_keys[3], (TOKENS, HEADS * HD), 1.0, 6.0, ((0, 32),))
    page_dest = draw_page_dest(jax.random.fold_in(arg_keys[6], 71), 0)
    doc_start = draw_doc_start(jax.random.fold_in(arg_keys[6], 71), 0)
    return dict(queries=queries, keys=keys, values=values, grad_out=grad_out, page_dest=page_dest, doc_start=doc_start)


def head_grads(query_h, key_h, value_h, cotan_h, visible, score_scale):
    scores = jnp.dot(query_h, key_h.T, preferred_element_type=jnp.float32) * score_scale
    scores = jnp.where(visible, scores, -jnp.inf)
    row_top = jnp.max(scores, axis=1, keepdims=True)
    weights = jnp.exp(scores - row_top)
    prob_low = (weights / jnp.sum(weights, axis=1, keepdims=True)).astype(jnp.bfloat16)
    attended = jnp.dot(prob_low, value_h, preferred_element_type=jnp.float32).astype(jnp.bfloat16)
    attended = lax.optimization_barrier(attended)
    row_dot = jnp.sum(cotan_h.astype(jnp.float32) * attended.astype(jnp.float32), axis=1, keepdims=True)
    grad_value = jnp.dot(prob_low.T, cotan_h, preferred_element_type=jnp.float32).astype(jnp.bfloat16)
    grad_prob = jnp.dot(cotan_h, value_h.T, preferred_element_type=jnp.float32)
    prob_kept = lax.optimization_barrier(prob_low)
    grad_score = (prob_kept.astype(jnp.float32) * (grad_prob - row_dot) * score_scale).astype(jnp.bfloat16)
    grad_query = jnp.dot(grad_score, key_h, preferred_element_type=jnp.float32).astype(jnp.bfloat16)
    grad_key = jnp.dot(grad_score.T, query_h, preferred_element_type=jnp.float32).astype(jnp.bfloat16)
    return grad_query, grad_key, grad_value


def reference(queries, keys, values, grad_out, page_dest, doc_start):
    score_scale = float(HD) ** -0.5
    page_range = jnp.arange(PAGES, dtype=jnp.int32)
    source = jnp.zeros((PAGES,), jnp.int32).at[page_dest].set(page_range)
    offsets = jnp.arange(PAGE, dtype=jnp.int32)
    positions = jnp.arange(SEG, dtype=jnp.int32)

    def one_bucket(bucket_index):
        slot_pages = lax.dynamic_slice_in_dim(source, bucket_index * SLOTS, SLOTS)
        token_rows = (slot_pages[:, None] * PAGE + offsets[None, :]).reshape(SEG)
        doc_slots = lax.dynamic_slice_in_dim(doc_start, bucket_index * SLOTS, SLOTS)
        token_start = jnp.repeat(doc_slots * PAGE, PAGE)
        visible = (positions[None, :] <= positions[:, None]) & (positions[None, :] >= token_start[:, None])
        query_b = jnp.take(queries, token_rows, axis=0).reshape(SEG, HEADS, HD)
        key_b = jnp.take(keys, token_rows, axis=0).reshape(SEG, HEADS, HD)
        value_b = jnp.take(values, token_rows, axis=0).reshape(SEG, HEADS, HD)
        cotan_b = jnp.take(grad_out, token_rows, axis=0).reshape(SEG, HEADS, HD)

        def one_head(head_index):
            pick_q = lax.dynamic_index_in_dim(query_b, head_index, 1, keepdims=False)
            pick_k = lax.dynamic_index_in_dim(key_b, head_index, 1, keepdims=False)
            pick_v = lax.dynamic_index_in_dim(value_b, head_index, 1, keepdims=False)
            pick_g = lax.dynamic_index_in_dim(cotan_b, head_index, 1, keepdims=False)
            return jnp.stack(head_grads(pick_q, pick_k, pick_v, pick_g, visible, score_scale))

        per_head = lax.map(one_head, jnp.arange(HEADS, dtype=jnp.int32))
        return jnp.transpose(per_head, (1, 2, 0, 3)).reshape(3, SEG, HEADS * HD)

    grads = lax.map(one_bucket, jnp.arange(N_BUCKET, dtype=jnp.int32))
    rows_all = (source[:, None] * PAGE + offsets[None, :]).reshape(TOKENS)
    results = []
    for which in range(3):
        flat = grads[:, which].reshape(TOKENS, HEADS * HD)
        results.append(jnp.zeros((TOKENS, HEADS * HD), jnp.bfloat16).at[rows_all].set(flat))
    return (results[0], results[1], results[2])
```

```python
import functools

import jax
import jax.numpy as jnp
from jax import lax
from jax.experimental import pallas as pl
from jax.experimental.pallas import tpu as pltpu
from jax.sharding import PartitionSpec as P

HD = 128
LOG2E = 1.4426950408889634
MESH = pl.DeviceIdType.MESH


def routing(page_dest, doc_start, bucket_index, head_index, n_bucket, n_head, block_slots):
    slots = n_bucket * n_head
    dest = page_dest.reshape(slots, n_bucket)
    dest_bucket = dest // slots
    arrival_slot = jnp.sum(jnp.where(dest_bucket == bucket_index, dest % slots, 0), axis=1)
    slot_range = jnp.arange(slots, dtype=jnp.int32)
    slot_order = jnp.sum(
        jnp.where(arrival_slot[:, None] == slot_range[None, :], slot_range[:, None], 0), axis=0
    )
    mine = lax.dynamic_index_in_dim(
        dest_bucket, bucket_index * n_head + head_index, 0, keepdims=False
    )
    page_range = jnp.arange(n_bucket, dtype=jnp.int32)
    pick = jnp.sum(jnp.where(mine[:, None] == page_range[None, :], page_range[:, None], 0), axis=0)
    starts = lax.dynamic_slice_in_dim(doc_start, bucket_index * slots, slots)
    starts = starts.reshape(slots // block_slots, block_slots)[:, 0]
    firsts = jnp.arange(slots // block_slots, dtype=jnp.int32) * block_slots
    hidden = jnp.where(firsts[None, :] >= starts[:, None], 0.0, -jnp.inf).astype(jnp.float32)
    return pick, mine, arrival_slot, slot_order, hidden.reshape(-1)


def dot_nt(a, b):
    return lax.dot_general(a, b, (((1,), (1,)), ((), ())), preferred_element_type=jnp.float32)


def dot(a, b):
    return jnp.dot(a, b, preferred_element_type=jnp.float32)


def kernel(
    n_bucket, n_head, heads, page, block,
    pick, mine, arrival, order, hidden,
    q_in, k_in, v_in, g_in,
    q_out, k_out, v_out,
    send, recv, back, home, stage, stage_back,
    q_s, k_s, v_s, g_s, k_t, dq, dk, dv, dk_sum, dv_sum,
    send_sem, recv_sem, back_sem, home_sem,
):
    n = n_bucket * n_head
    me = lax.axis_index("bucket") * n_head + lax.axis_index("head")
    seg = n * page
    blocks = seg // block
    scale = float(HD) ** (-0.5)

    barrier = pltpu.get_barrier_semaphore()

    @pl.loop(1, n)
    def _(step):
        d = lax.rem(me + step, n)
        pl.semaphore_signal(
            barrier, inc=1, device_id=(d // n_head, lax.rem(d, n_head)), device_id_type=MESH
        )

    def pack(h, d, where):
        from_page = pick[d // n_head]
        column = pl.multiple_of((lax.rem(d, n_head) * heads + h) * HD, HD)
        for a, src in enumerate((q_in, k_in, v_in, g_in)):
            where[h, d, pl.ds(a * page, page), :] = src[from_page, :, pl.ds(column, HD)]

    pl.semaphore_wait(barrier, n - 1)

    @pl.loop(0, heads)
    def _(h):
        @pl.loop(1, n)
        def _(step):
            d = lax.rem(me + step, n)
            pack(h, d, send)
            pltpu.make_async_remote_copy(
                src_ref=send.at[h, d],
                dst_ref=recv.at[h, me],
                send_sem=send_sem.at[h],
                recv_sem=recv_sem.at[h],
                device_id=(d // n_head, lax.rem(d, n_head)),
                device_id_type=MESH,
            ).start()

        pack(h, me, recv)

    key_row = lax.broadcasted_iota(jnp.int32, (block, block), 0)
    query_col = lax.broadcasted_iota(jnp.int32, (block, block), 1)
    causal = key_row <= query_col

    def attend(i):
        rows = (i + 1) * block
        here = pl.ds(i * block, block)
        q_b = q_s[here, :]
        g_b = g_s[here, :]
        s = dot_nt(k_s[pl.ds(0, rows), :], q_b)
        parts = []
        for j in range(i):
            parts.append(s[j * block : (j + 1) * block] + hidden[i * blocks + j])
        parts.append(jnp.where(causal, s[i * block :], -jnp.inf))
        s = jnp.concatenate(parts, axis=0) if i else parts[0]
        top = jnp.max(s, axis=0, keepdims=True)
        w = jnp.exp2((s - top) * (scale * LOG2E))
        p = (w * (1.0 / jnp.sum(w, axis=0, keepdims=True))).astype(jnp.bfloat16)
        gp = dot_nt(v_s[pl.ds(0, rows), :], g_b)
        p32 = p.astype(jnp.float32)
        row_dot = jnp.sum(p32 * gp, axis=0, keepdims=True)
        gs = (p32 * ((gp - row_dot) * scale)).astype(jnp.bfloat16)
        if i == blocks - 1:
            dv_sum[...] = dot(p, g_b)
            dk_sum[...] = dot(gs, q_b)
        else:
            dv_sum[pl.ds(0, rows), :] += dot(p, g_b)
            dk_sum[pl.ds(0, rows), :] += dot(gs, q_b)
        gq = dot(k_t[:, pl.ds(0, rows)], gs).T.reshape(block // page, page, HD)
        dq[pl.ds(i * (block // page), block // page)] = gq.astype(jnp.bfloat16)

    def wait_all(ref, h, sem):
        part = ref.at[h, pl.ds(0, n - 1)]
        pltpu.make_async_copy(part, part, sem.at[h]).wait()

    def pack_back(h, d, at, where):
        slot = arrival[d]
        for a, src in enumerate((dq, dk, dv)):
            where[h, at, pl.ds(a * page, page), :] = src[slot]

    @pl.loop(0, heads)
    def _(h):
        wait_all(recv, h, recv_sem)

        @pl.loop(0, n)
        def _(s):
            stage[s] = recv[h, s]

        @pl.loop(0, n)
        def _(s):
            src = order[s]
            to = pl.ds(pl.multiple_of(s * page, page), page)
            for a, dst in enumerate((q_s, k_s, v_s, g_s)):
                dst[to, :] = stage[src, pl.ds(a * page, page), :]

        k_t[...] = k_s[...].T
        for i in reversed(range(blocks)):
            attend(i)
        dk[...] = dk_sum[...].reshape(n, page, HD).astype(jnp.bfloat16)
        dv[...] = dv_sum[...].reshape(n, page, HD).astype(jnp.bfloat16)

        @pl.loop(1, n)
        def _(step):
            d = lax.rem(me + step, n)
            pack_back(h, d, d, back)
            pltpu.make_async_remote_copy(
                src_ref=back.at[h, d],
                dst_ref=home.at[h, me],
                send_sem=back_sem.at[h],
                recv_sem=home_sem.at[h],
                device_id=(d // n_head, lax.rem(d, n_head)),
                device_id_type=MESH,
            ).start()

        pack_back(h, me, me, home)

    @pl.loop(0, heads)
    def _(h):
        wait_all(home, h, home_sem)

        @pl.loop(0, n)
        def _(s):
            stage_back[s] = home[h, s]

        @pl.loop(0, n)
        def _(t):
            p = t // n_head
            group = lax.rem(t, n_head)
            src = mine[p] * n_head + group
            to = pl.ds(pl.multiple_of(p * page, page), page)
            column = pl.ds(pl.multiple_of((group * heads + h) * HD, HD), HD)
            for a, dst in enumerate((q_out, k_out, v_out)):
                dst[to, column] = stage_back[src, pl.ds(a * page, page), :]

    @pl.loop(0, heads)
    def _(h):
        wait_all(send, h, send_sem)
        wait_all(back, h, back_sem)


def shards(queries, keys, values, grad_out, page_dest, doc_start):
    n_bucket = lax.axis_size("bucket")
    n_head = lax.axis_size("head")
    n = n_bucket * n_head
    tok_dev, width = queries.shape
    page = tok_dev // n_bucket
    heads = width // n_head // HD
    seg = n * page
    block_slots = 2 * n_bucket
    block = block_slots * page
    tables = routing(
        page_dest, doc_start, lax.axis_index("bucket"), lax.axis_index("head"),
        n_bucket, n_head, block_slots,
    )
    low = jnp.bfloat16
    back_rows = -(-3 * page // 16) * 16
    smem = pl.BlockSpec(memory_space=pltpu.SMEM)
    vmem = pl.BlockSpec(memory_space=pltpu.VMEM)
    pairs = heads * seg * seg // 2
    return pl.pallas_call(
        functools.partial(kernel, n_bucket, n_head, heads, page, block),
        out_shape=[jax.ShapeDtypeStruct((tok_dev, width), low)] * 3,
        in_specs=[smem] * 5 + [vmem] * 4,
        out_specs=[vmem] * 3,
        scratch_shapes=[
            pltpu.VMEM((heads, n, 4 * page, HD), low),
            pltpu.VMEM((heads, n, 4 * page, HD), low),
            pltpu.VMEM((heads, n, back_rows, HD), low),
            pltpu.VMEM((heads, n, back_rows, HD), low),
            pltpu.VMEM((n, 4 * page, HD), low),
            pltpu.VMEM((n, back_rows, HD), low),
            pltpu.VMEM((seg, HD), low),
            pltpu.VMEM((seg, HD), low),
            pltpu.VMEM((seg, HD), low),
            pltpu.VMEM((seg, HD), low),
            pltpu.VMEM((HD, seg), low),
            pltpu.VMEM((n, page, HD), low),
            pltpu.VMEM((n, page, HD), low),
            pltpu.VMEM((n, page, HD), low),
            pltpu.VMEM((seg, HD), jnp.float32),
            pltpu.VMEM((seg, HD), jnp.float32),
            pltpu.SemaphoreType.DMA((heads,)),
            pltpu.SemaphoreType.DMA((heads,)),
            pltpu.SemaphoreType.DMA((heads,)),
            pltpu.SemaphoreType.DMA((heads,)),
        ],
        compiler_params=pltpu.CompilerParams(
            collective_id=0, has_side_effects=True, vmem_limit_bytes=56 * 1024 * 1024
        ),
        cost_estimate=pl.CostEstimate(
            flops=10 * pairs * HD, bytes_accessed=14 * tok_dev * width, transcendentals=pairs
        ),
    )(*tables, *(a.reshape(n_bucket, page, width) for a in (queries, keys, values, grad_out)))


def solution(mesh):
    split = P(("bucket", "head"), None)
    return jax.shard_map(
        shards,
        mesh=mesh,
        in_specs=(split, split, split, split, P(), P()),
        out_specs=(split, split, split),
        check_vma=False,
    )
```

```python
import functools

import jax
import jax.numpy as jnp
from jax import lax
from jax.experimental import pallas as pl
from jax.experimental.pallas import tpu as pltpu
from jax.sharding import PartitionSpec as P

HD = 128
LOG2E = 1.4426950408889634
MESH = pl.DeviceIdType.MESH


def routing(page_dest, doc_start, bucket_index, head_index, n_bucket, n_head, block_slots):
    slots = n_bucket * n_head
    dest = page_dest.reshape(slots, n_bucket)
    dest_bucket = dest // slots
    arrival_slot = jnp.sum(jnp.where(dest_bucket == bucket_index, dest % slots, 0), axis=1)
    slot_range = jnp.arange(slots, dtype=jnp.int32)
    slot_order = jnp.sum(
        jnp.where(arrival_slot[:, None] == slot_range[None, :], slot_range[:, None], 0), axis=0
    )
    mine = lax.dynamic_index_in_dim(
        dest_bucket, bucket_index * n_head + head_index, 0, keepdims=False
    )
    page_range = jnp.arange(n_bucket, dtype=jnp.int32)
    pick = jnp.sum(jnp.where(mine[:, None] == page_range[None, :], page_range[:, None], 0), axis=0)
    starts = lax.dynamic_slice_in_dim(doc_start, bucket_index * slots, slots)
    starts = starts.reshape(slots // block_slots, block_slots)[:, 0]
    firsts = jnp.arange(slots // block_slots, dtype=jnp.int32) * block_slots
    hidden = (firsts[None, :] < starts[:, None]).astype(jnp.int32)
    return jnp.concatenate([pick, mine, arrival_slot, slot_order, hidden.reshape(-1)])


def dot_nt(a, b):
    return lax.dot_general(a, b, (((1,), (1,)), ((), ())), preferred_element_type=jnp.float32)


def dot(a, b):
    return jnp.dot(a, b, preferred_element_type=jnp.float32)


def kernel(
    n_bucket, n_head, heads, page, block,
    table,
    q_in, k_in, v_in, g_in,
    q_out, k_out, v_out,
    send, recv, back, home, stage, stage_back,
    q_s, k_s, v_s, g_s, k_t, dq, dk, dv, dk_sum, dv_sum,
    send_sem, recv_sem, back_sem, home_sem,
):
    n = n_bucket * n_head
    me = lax.axis_index("bucket") * n_head + lax.axis_index("head")
    seg = n * page
    blocks = seg // block
    scale = float(HD) ** (-0.5)

    mine_at = n_bucket
    arrival_at = 2 * n_bucket
    order_at = arrival_at + n
    hidden_at = order_at + n

    barrier = pltpu.get_barrier_semaphore()

    @pl.loop(1, n)
    def _(step):
        d = lax.rem(me + step, n)
        pl.semaphore_signal(
            barrier, inc=1, device_id=(d // n_head, lax.rem(d, n_head)), device_id_type=MESH
        )

    def pack(h, d, where):
        from_page = table[d // n_head]
        column = pl.multiple_of((lax.rem(d, n_head) * heads + h) * HD, HD)
        for a, src in enumerate((q_in, k_in, v_in, g_in)):
            where[h, d, pl.ds(a * page, page), :] = src[from_page, :, pl.ds(column, HD)]

    pl.semaphore_wait(barrier, n - 1)

    @pl.loop(0, heads)
    def _(h):
        @pl.loop(1, n)
        def _(step):
            d = lax.rem(me + step, n)
            pack(h, d, send)
            pltpu.make_async_remote_copy(
                src_ref=send.at[h, d],
                dst_ref=recv.at[h, me],
                send_sem=send_sem.at[h],
                recv_sem=recv_sem.at[h],
                device_id=(d // n_head, lax.rem(d, n_head)),
                device_id_type=MESH,
            ).start()

        pack(h, me, recv)

    key_row = lax.broadcasted_iota(jnp.int32, (block, block), 0)
    query_col = lax.broadcasted_iota(jnp.int32, (block, block), 1)
    causal = key_row <= query_col

    def attend(i):
        rows = (i + 1) * block
        here = pl.ds(i * block, block)
        q_b = q_s[here, :]
        g_b = g_s[here, :]
        s = dot_nt(k_s[pl.ds(0, rows), :], q_b)
        parts = []
        for j in range(i):
            lower = table[hidden_at + i * blocks + j].astype(jnp.float32) * -3e38
            parts.append(s[j * block : (j + 1) * block] + lower)
        parts.append(jnp.where(causal, s[i * block :], -jnp.inf))
        s = jnp.concatenate(parts, axis=0) if i else parts[0]
        top = jnp.max(s, axis=0, keepdims=True)
        w = jnp.exp2((s - top) * (scale * LOG2E))
        p = (w * (1.0 / jnp.sum(w, axis=0, keepdims=True))).astype(jnp.bfloat16)
        gp = dot_nt(v_s[pl.ds(0, rows), :], g_b)
        p32 = p.astype(jnp.float32)
        row_dot = jnp.sum(p32 * gp, axis=0, keepdims=True)
        gs = (p32 * ((gp - row_dot) * scale)).astype(jnp.bfloat16)
        if i == blocks - 1:
            dv_sum[...] = dot(p, g_b)
            dk_sum[...] = dot(gs, q_b)
        else:
            dv_sum[pl.ds(0, rows), :] += dot(p, g_b)
            dk_sum[pl.ds(0, rows), :] += dot(gs, q_b)
        gq = dot(k_t[:, pl.ds(0, rows)], gs).T.reshape(block // page, page, HD)
        dq[pl.ds(i * (block // page), block // page)] = gq.astype(jnp.bfloat16)

    def wait_all(ref, h, sem):
        part = ref.at[h, pl.ds(0, n - 1)]
        pltpu.make_async_copy(part, part, sem.at[h]).wait()

    def pack_back(h, d, at, where):
        slot = table[arrival_at + d]
        for a, src in enumerate((dq, dk, dv)):
            where[h, at, pl.ds(a * page, page), :] = src[slot]

    def send_back(h):
        @pl.loop(1, n)
        def _(step):
            d = lax.rem(me + step, n)
            pltpu.make_async_remote_copy(
                src_ref=back.at[h, d],
                dst_ref=home.at[h, me],
                send_sem=back_sem.at[h],
                recv_sem=home_sem.at[h],
                device_id=(d // n_head, lax.rem(d, n_head)),
                device_id_type=MESH,
            ).start()

    @pl.loop(0, heads)
    def _(h):
        wait_all(recv, h, recv_sem)

        @pl.when(h == heads - 1)
        def _():
            @pl.loop(0, heads - 1)
            def _(done):
                send_back(done)

        @pl.loop(0, n)
        def _(s):
            stage[s] = recv[h, s]

        @pl.loop(0, n)
        def _(s):
            src = table[order_at + s]
            to = pl.ds(pl.multiple_of(s * page, page), page)
            for a, dst in enumerate((q_s, k_s, v_s, g_s)):
                dst[to, :] = stage[src, pl.ds(a * page, page), :]

        k_t[...] = k_s[...].T
        for i in reversed(range(blocks)):
            attend(i)
        dk[...] = dk_sum[...].reshape(n, page, HD).astype(jnp.bfloat16)
        dv[...] = dv_sum[...].reshape(n, page, HD).astype(jnp.bfloat16)

        @pl.loop(1, n)
        def _(step):
            d = lax.rem(me + step, n)
            pack_back(h, d, d, back)

        pack_back(h, me, me, home)

    send_back(heads - 1)

    @pl.loop(0, heads)
    def _(h):
        wait_all(home, h, home_sem)

        @pl.loop(0, n)
        def _(s):
            stage_back[s] = home[h, s]

        @pl.loop(0, n)
        def _(t):
            p = t // n_head
            group = lax.rem(t, n_head)
            src = table[mine_at + p] * n_head + group
            to = pl.ds(pl.multiple_of(p * page, page), page)
            column = pl.ds(pl.multiple_of((group * heads + h) * HD, HD), HD)
            for a, dst in enumerate((q_out, k_out, v_out)):
                dst[to, column] = stage_back[src, pl.ds(a * page, page), :]

    @pl.loop(0, heads)
    def _(h):
        wait_all(send, h, send_sem)
        wait_all(back, h, back_sem)


def shards(queries, keys, values, grad_out, page_dest, doc_start):
    n_bucket = lax.axis_size("bucket")
    n_head = lax.axis_size("head")
    n = n_bucket * n_head
    tok_dev, width = queries.shape
    page = tok_dev // n_bucket
    heads = width // n_head // HD
    seg = n * page
    block_slots = 2 * n_bucket
    block = block_slots * page
    table = routing(
        page_dest, doc_start, lax.axis_index("bucket"), lax.axis_index("head"),
        n_bucket, n_head, block_slots,
    )
    low = jnp.bfloat16
    back_rows = -(-3 * page // 16) * 16
    smem = pl.BlockSpec(memory_space=pltpu.SMEM)
    vmem = pl.BlockSpec(memory_space=pltpu.VMEM)
    pairs = heads * seg * seg // 2
    return pl.pallas_call(
        functools.partial(kernel, n_bucket, n_head, heads, page, block),
        out_shape=[jax.ShapeDtypeStruct((tok_dev, width), low)] * 3,
        in_specs=[smem] + [vmem] * 4,
        out_specs=[vmem] * 3,
        scratch_shapes=[
            pltpu.VMEM((heads, n, 4 * page, HD), low),
            pltpu.VMEM((heads, n, 4 * page, HD), low),
            pltpu.VMEM((heads, n, back_rows, HD), low),
            pltpu.VMEM((heads, n, back_rows, HD), low),
            pltpu.VMEM((n, 4 * page, HD), low),
            pltpu.VMEM((n, back_rows, HD), low),
            pltpu.VMEM((seg, HD), low),
            pltpu.VMEM((seg, HD), low),
            pltpu.VMEM((seg, HD), low),
            pltpu.VMEM((seg, HD), low),
            pltpu.VMEM((HD, seg), low),
            pltpu.VMEM((n, page, HD), low),
            pltpu.VMEM((n, page, HD), low),
            pltpu.VMEM((n, page, HD), low),
            pltpu.VMEM((seg, HD), jnp.float32),
            pltpu.VMEM((seg, HD), jnp.float32),
            pltpu.SemaphoreType.DMA((heads,)),
            pltpu.SemaphoreType.DMA((heads,)),
            pltpu.SemaphoreType.DMA((heads,)),
            pltpu.SemaphoreType.DMA((heads,)),
        ],
        compiler_params=pltpu.CompilerParams(
            collective_id=0, has_side_effects=True, vmem_limit_bytes=56 * 1024 * 1024
        ),
        cost_estimate=pl.CostEstimate(
            flops=10 * pairs * HD, bytes_accessed=14 * tok_dev * width, transcendentals=pairs
        ),
    )(table, *(a.reshape(n_bucket, page, width) for a in (queries, keys, values, grad_out)))


def solution(mesh):
    split = P(("bucket", "head"), None)
    return jax.shard_map(
        shards,
        mesh=mesh,
        in_specs=(split, split, split, split, P(), P()),
        out_specs=(split, split, split),
        check_vma=False,
    )
```

```python
import functools

import jax
import jax.numpy as jnp
from jax import lax
from jax.experimental import pallas as pl
from jax.experimental.pallas import tpu as pltpu
from jax.sharding import PartitionSpec as P

HD = 128
LOG2E = 1.4426950408889634
MESH = pl.DeviceIdType.MESH


def routing(page_dest, doc_start, bucket_index, head_index, n_bucket, n_head, block_slots):
    slots = n_bucket * n_head
    dest = page_dest.reshape(slots, n_bucket)
    dest_bucket = dest // slots
    arrival_slot = jnp.sum(jnp.where(dest_bucket == bucket_index, dest % slots, 0), axis=1)
    slot_range = jnp.arange(slots, dtype=jnp.int32)
    slot_order = jnp.sum(
        jnp.where(arrival_slot[:, None] == slot_range[None, :], slot_range[:, None], 0), axis=0
    )
    mine = lax.dynamic_index_in_dim(
        dest_bucket, bucket_index * n_head + head_index, 0, keepdims=False
    )
    page_range = jnp.arange(n_bucket, dtype=jnp.int32)
    pick = jnp.sum(jnp.where(mine[:, None] == page_range[None, :], page_range[:, None], 0), axis=0)
    starts = lax.dynamic_slice_in_dim(doc_start, bucket_index * slots, slots)
    starts = starts.reshape(slots // block_slots, block_slots)[:, 0]
    firsts = jnp.arange(slots // block_slots, dtype=jnp.int32) * block_slots
    hidden = (firsts[None, :] < starts[:, None]).astype(jnp.int32)
    return mine, jnp.concatenate([pick, arrival_slot, slot_order, hidden.reshape(-1)])


def dot_nt(a, b):
    return lax.dot_general(a, b, (((1,), (1,)), ((), ())), preferred_element_type=jnp.float32)


def dot(a, b):
    return jnp.dot(a, b, preferred_element_type=jnp.float32)


def kernel(
    n_bucket, n_head, heads, page, block,
    table,
    q_hbm, k_hbm, v_hbm, g_hbm,
    home,
    q_in, k_in, v_in, g_in,
    send, recv, back, stage,
    q_s, k_s, v_s, g_s, k_t, dq, dk, dv, dk_sum, dv_sum,
    send_sem, recv_sem, back_sem, home_sem, own_sem, load_sem,
):
    n = n_bucket * n_head
    me = lax.axis_index("bucket") * n_head + lax.axis_index("head")
    seg = n * page
    blocks = seg // block
    scale = float(HD) ** (-0.5)

    arrival_at = n_bucket
    order_at = arrival_at + n
    hidden_at = order_at + n

    loads = [
        pltpu.make_async_copy(src, dst, load_sem.at[a])
        for a, (src, dst) in enumerate(
            ((q_hbm, q_in), (k_hbm, k_in), (v_hbm, v_in), (g_hbm, g_in))
        )
    ]
    for load in loads:
        load.start()

    barrier = pltpu.get_barrier_semaphore()

    @pl.loop(1, n)
    def _(step):
        d = lax.rem(me + step, n)
        pl.semaphore_signal(
            barrier, inc=1, device_id=(d // n_head, lax.rem(d, n_head)), device_id_type=MESH
        )

    def pack(h, d, where):
        from_page = table[d // n_head]
        column = pl.multiple_of((lax.rem(d, n_head) * heads + h) * HD, HD)
        for a, src in enumerate((q_in, k_in, v_in, g_in)):
            where[h, d, pl.ds(a * page, page), :] = src[from_page, :, pl.ds(column, HD)]

    pl.semaphore_wait(barrier, n - 1)
    for load in loads:
        load.wait()

    @pl.loop(0, heads)
    def _(h):
        @pl.loop(1, n)
        def _(step):
            d = lax.rem(me + step, n)
            pack(h, d, send)
            pltpu.make_async_remote_copy(
                src_ref=send.at[h, d],
                dst_ref=recv.at[h, me],
                send_sem=send_sem.at[h],
                recv_sem=recv_sem.at[h],
                device_id=(d // n_head, lax.rem(d, n_head)),
                device_id_type=MESH,
            ).start()

        pack(h, me, recv)

    key_row = lax.broadcasted_iota(jnp.int32, (block, block), 0)
    query_col = lax.broadcasted_iota(jnp.int32, (block, block), 1)
    causal = key_row <= query_col

    def attend(i):
        rows = (i + 1) * block
        here = pl.ds(i * block, block)
        q_b = q_s[here, :]
        g_b = g_s[here, :]
        s = dot_nt(k_s[pl.ds(0, rows), :], q_b)
        parts = []
        for j in range(i):
            lower = table[hidden_at + i * blocks + j].astype(jnp.float32) * -3e38
            parts.append(s[j * block : (j + 1) * block] + lower)
        parts.append(jnp.where(causal, s[i * block :], -jnp.inf))
        s = jnp.concatenate(parts, axis=0) if i else parts[0]
        top = jnp.max(s, axis=0, keepdims=True)
        w = jnp.exp2((s - top) * (scale * LOG2E))
        p = (w * (1.0 / jnp.sum(w, axis=0, keepdims=True))).astype(jnp.bfloat16)
        gp = dot_nt(v_s[pl.ds(0, rows), :], g_b)
        p32 = p.astype(jnp.float32)
        row_dot = jnp.sum(p32 * gp, axis=0, keepdims=True)
        gs = (p32 * ((gp - row_dot) * scale)).astype(jnp.bfloat16)
        if i == blocks - 1:
            dv_sum[...] = dot(p, g_b)
            dk_sum[...] = dot(gs, q_b)
        else:
            dv_sum[pl.ds(0, rows), :] += dot(p, g_b)
            dk_sum[pl.ds(0, rows), :] += dot(gs, q_b)
        gq = dot(k_t[:, pl.ds(0, rows)], gs).T.reshape(block // page, page, HD)
        dq[pl.ds(i * (block // page), block // page)] = gq.astype(jnp.bfloat16)

    def wait_all(ref, h, sem):
        part = ref.at[h, pl.ds(0, n - 1)]
        pltpu.make_async_copy(part, part, sem.at[h]).wait()

    def pack_back(h, d):
        slot = table[arrival_at + d]
        for a, src in enumerate((dq, dk, dv)):
            back[h, d, pl.ds(a * page, page), :] = src[slot]

    @pl.loop(0, heads)
    def _(h):
        wait_all(recv, h, recv_sem)

        @pl.loop(0, n)
        def _(s):
            stage[s] = recv[h, s]

        @pl.loop(0, n)
        def _(s):
            src = table[order_at + s]
            to = pl.ds(pl.multiple_of(s * page, page), page)
            for a, dst in enumerate((q_s, k_s, v_s, g_s)):
                dst[to, :] = stage[src, pl.ds(a * page, page), :]

        k_t[...] = k_s[...].T
        for i in reversed(range(blocks)):
            attend(i)
        dk[...] = dk_sum[...].reshape(n, page, HD).astype(jnp.bfloat16)
        dv[...] = dv_sum[...].reshape(n, page, HD).astype(jnp.bfloat16)

        @pl.loop(1, n)
        def _(step):
            d = lax.rem(me + step, n)
            pack_back(h, d)
            pltpu.make_async_remote_copy(
                src_ref=back.at[h, d],
                dst_ref=home.at[h, me],
                send_sem=back_sem.at[h],
                recv_sem=home_sem.at[h],
                device_id=(d // n_head, lax.rem(d, n_head)),
                device_id_type=MESH,
            ).start()

        pack_back(h, me)
        pltpu.make_async_copy(back.at[h, me], home.at[h, me], own_sem.at[h]).start()

    @pl.loop(0, heads)
    def _(h):
        wait_all(home, h, home_sem)
        pltpu.make_async_copy(back.at[h, me], home.at[h, me], own_sem.at[h]).wait()
        wait_all(send, h, send_sem)
        wait_all(back, h, back_sem)


def deliver(heads, page, mine, home, q_out, k_out, v_out):
    for p in range(mine.shape[0]):
        bucket = mine[p]
        for h in range(heads):
            for a, dst in enumerate((q_out, k_out, v_out)):
                dst[p, :, pl.ds(h * HD, HD)] = home[h, bucket, 0, pl.ds(a * page, page), :]


def shards(queries, keys, values, grad_out, page_dest, doc_start):
    n_bucket = lax.axis_size("bucket")
    n_head = lax.axis_size("head")
    n = n_bucket * n_head
    tok_dev, width = queries.shape
    page = tok_dev // n_bucket
    heads = width // n_head // HD
    seg = n * page
    block_slots = 2 * n_bucket
    block = block_slots * page
    mine, table = routing(
        page_dest, doc_start, lax.axis_index("bucket"), lax.axis_index("head"),
        n_bucket, n_head, block_slots,
    )
    low = jnp.bfloat16
    back_rows = -(-3 * page // 16) * 16
    smem = pl.BlockSpec(memory_space=pltpu.SMEM)
    hbm = pl.BlockSpec(memory_space=pl.ANY)
    pairs = heads * seg * seg // 2
    home = pl.pallas_call(
        functools.partial(kernel, n_bucket, n_head, heads, page, block),
        out_shape=jax.ShapeDtypeStruct((heads, n, back_rows, HD), low),
        in_specs=[smem] + [hbm] * 4,
        out_specs=hbm,
        scratch_shapes=[
            pltpu.VMEM((n_bucket, page, width), low),
            pltpu.VMEM((n_bucket, page, width), low),
            pltpu.VMEM((n_bucket, page, width), low),
            pltpu.VMEM((n_bucket, page, width), low),
            pltpu.VMEM((heads, n, 4 * page, HD), low),
            pltpu.VMEM((heads, n, 4 * page, HD), low),
            pltpu.VMEM((heads, n, back_rows, HD), low),
            pltpu.VMEM((n, 4 * page, HD), low),
            pltpu.VMEM((seg, HD), low),
            pltpu.VMEM((seg, HD), low),
            pltpu.VMEM((seg, HD), low),
            pltpu.VMEM((seg, HD), low),
            pltpu.VMEM((HD, seg), low),
            pltpu.VMEM((n, page, HD), low),
            pltpu.VMEM((n, page, HD), low),
            pltpu.VMEM((n, page, HD), low),
            pltpu.VMEM((seg, HD), jnp.float32),
            pltpu.VMEM((seg, HD), jnp.float32),
            pltpu.SemaphoreType.DMA((heads,)),
            pltpu.SemaphoreType.DMA((heads,)),
            pltpu.SemaphoreType.DMA((heads,)),
            pltpu.SemaphoreType.DMA((heads,)),
            pltpu.SemaphoreType.DMA((heads,)),
            pltpu.SemaphoreType.DMA((4,)),
        ],
        compiler_params=pltpu.CompilerParams(
            collective_id=0, has_side_effects=True, vmem_limit_bytes=56 * 1024 * 1024
        ),
        cost_estimate=pl.CostEstimate(
            flops=10 * pairs * HD, bytes_accessed=14 * tok_dev * width, transcendentals=pairs
        ),
    )(table, *(a.reshape(n_bucket, page, width) for a in (queries, keys, values, grad_out)))
    outs = pl.pallas_call(
        functools.partial(deliver, heads, page),
        grid=(n_head,),
        out_shape=[jax.ShapeDtypeStruct((n_bucket, page, width), low)] * 3,
        in_specs=[
            smem,
            pl.BlockSpec((heads, n_bucket, 1, back_rows, HD), lambda g: (0, 0, g, 0, 0)),
        ],
        out_specs=[pl.BlockSpec((n_bucket, page, heads * HD), lambda g: (0, 0, g))] * 3,
    )(mine, home.reshape(heads, n_bucket, n_head, back_rows, HD))
    return tuple(a.reshape(tok_dev, width) for a in outs)


def solution(mesh):
    split = P(("bucket", "head"), None)
    return jax.shard_map(
        shards,
        mesh=mesh,
        in_specs=(split, split, split, split, P(), P()),
        out_specs=(split, split, split),
        check_vma=False,
    )
```

```python
import functools

import jax
import jax.numpy as jnp
from jax import lax
from jax.experimental import pallas as pl
from jax.experimental.pallas import tpu as pltpu
from jax.sharding import PartitionSpec as P

HD = 128
LOG2E = 1.4426950408889634
MESH = pl.DeviceIdType.MESH


def routing(page_dest, doc_start, bucket_index, head_index, n_bucket, n_head, block_slots):
    slots = n_bucket * n_head
    dest = page_dest.reshape(slots, n_bucket)
    dest_bucket = dest // slots
    arrival_slot = jnp.sum(jnp.where(dest_bucket == bucket_index, dest % slots, 0), axis=1)
    slot_range = jnp.arange(slots, dtype=jnp.int32)
    slot_order = jnp.sum(
        jnp.where(arrival_slot[:, None] == slot_range[None, :], slot_range[:, None], 0), axis=0
    )
    mine = lax.dynamic_index_in_dim(
        dest_bucket, bucket_index * n_head + head_index, 0, keepdims=False
    )
    page_range = jnp.arange(n_bucket, dtype=jnp.int32)
    pick = jnp.sum(jnp.where(mine[:, None] == page_range[None, :], page_range[:, None], 0), axis=0)
    starts = lax.dynamic_slice_in_dim(doc_start, bucket_index * slots, slots)
    starts = starts.reshape(slots // block_slots, block_slots)[:, 0]
    firsts = jnp.arange(slots // block_slots, dtype=jnp.int32) * block_slots
    hidden = (firsts[None, :] < starts[:, None]).astype(jnp.int32)
    return mine, jnp.concatenate([pick, arrival_slot, slot_order, hidden.reshape(-1)])


def dot_nt(a, b):
    return lax.dot_general(a, b, (((1,), (1,)), ((), ())), preferred_element_type=jnp.float32)


def dot(a, b):
    return jnp.dot(a, b, preferred_element_type=jnp.float32)


def kernel(
    n_bucket, n_head, heads, page, block,
    table,
    q_hbm, k_hbm, v_hbm, g_hbm,
    home,
    q_in, k_in, v_in, g_in,
    send, recv, back, stage,
    q_s, k_s, v_s, g_s, k_t, dq, dk, dv, dk_sum, dv_sum,
    send_sem, recv_sem, back_sem, home_sem, own_sem, load_sem,
):
    n = n_bucket * n_head
    me = lax.axis_index("bucket") * n_head + lax.axis_index("head")
    seg = n * page
    blocks = seg // block
    scale = float(HD) ** (-0.5)

    arrival_at = n_bucket
    order_at = arrival_at + n
    hidden_at = order_at + n

    loads = [
        pltpu.make_async_copy(src, dst, load_sem.at[a])
        for a, (src, dst) in enumerate(
            ((q_hbm, q_in), (k_hbm, k_in), (v_hbm, v_in), (g_hbm, g_in))
        )
    ]
    for load in loads:
        load.start()

    barrier = pltpu.get_barrier_semaphore()

    @pl.loop(1, n)
    def _(step):
        d = lax.rem(me + step, n)
        pl.semaphore_signal(
            barrier, inc=1, device_id=(d // n_head, lax.rem(d, n_head)), device_id_type=MESH
        )

    def pack(h, d, where):
        from_page = table[d // n_head]
        column = pl.multiple_of((lax.rem(d, n_head) * heads + h) * HD, HD)
        for a, src in enumerate((q_in, k_in, v_in, g_in)):
            where[h, d, pl.ds(a * page, page), :] = src[from_page, :, pl.ds(column, HD)]

    pl.semaphore_wait(barrier, n - 1)
    for load in loads:
        load.wait()

    @pl.loop(0, heads)
    def _(h):
        @pl.loop(1, n)
        def _(step):
            d = lax.rem(me + step, n)
            pack(h, d, send)
            pltpu.make_async_remote_copy(
                src_ref=send.at[h, d],
                dst_ref=recv.at[h, me],
                send_sem=send_sem.at[h],
                recv_sem=recv_sem.at[h],
                device_id=(d // n_head, lax.rem(d, n_head)),
                device_id_type=MESH,
            ).start()

        pack(h, me, recv)

    key_row = lax.broadcasted_iota(jnp.int32, (block, block), 0)
    query_col = lax.broadcasted_iota(jnp.int32, (block, block), 1)
    causal = key_row <= query_col

    def attend(i):
        rows = (i + 1) * block
        here = pl.ds(i * block, block)
        q_b = q_s[here, :]
        g_b = g_s[here, :]
        s = dot_nt(k_s[pl.ds(0, rows), :], q_b)
        parts = []
        for j in range(i):
            lower = table[hidden_at + i * blocks + j].astype(jnp.float32) * -3e38
            parts.append(s[j * block : (j + 1) * block] + lower)
        parts.append(jnp.where(causal, s[i * block :], -jnp.inf))
        s = jnp.concatenate(parts, axis=0) if i else parts[0]
        top = jnp.max(s, axis=0, keepdims=True)
        w = jnp.exp2((s - top) * (scale * LOG2E))
        p = (w * (1.0 / jnp.sum(w, axis=0, keepdims=True))).astype(jnp.bfloat16)
        gp = dot_nt(v_s[pl.ds(0, rows), :], g_b)
        p32 = p.astype(jnp.float32)
        row_dot = jnp.sum(p32 * gp, axis=0, keepdims=True)
        gs = (p32 * ((gp - row_dot) * scale)).astype(jnp.bfloat16)
        if i == blocks - 1:
            dv_sum[...] = dot(p, g_b)
            dk_sum[...] = dot(gs, q_b)
        else:
            dv_sum[pl.ds(0, rows), :] += dot(p, g_b)
            dk_sum[pl.ds(0, rows), :] += dot(gs, q_b)
        gq = dot(k_t[:, pl.ds(0, rows)], gs).T.reshape(block // page, page, HD)
        dq[pl.ds(i * (block // page), block // page)] = gq.astype(jnp.bfloat16)

    def wait_all(ref, h, sem):
        part = ref.at[h, pl.ds(0, n - 1)]
        pltpu.make_async_copy(part, part, sem.at[h]).wait()

    def pack_back(h, d):
        slot = table[arrival_at + d]
        for a, src in enumerate((dq, dk, dv)):
            back[h, d, pl.ds(a * page, page), :] = src[slot]

    @pl.loop(0, heads)
    def _(h):
        wait_all(recv, h, recv_sem)

        @pl.loop(0, n)
        def _(s):
            stage[s] = recv[h, s]

        @pl.loop(0, n)
        def _(s):
            src = table[order_at + s]
            to = pl.ds(pl.multiple_of(s * page, page), page)
            for a, dst in enumerate((q_s, k_s, v_s, g_s)):
                dst[to, :] = stage[src, pl.ds(a * page, page), :]

        k_t[...] = k_s[...].T
        for i in reversed(range(blocks)):
            attend(i)
        dk[...] = dk_sum[...].reshape(n, page, HD).astype(jnp.bfloat16)
        dv[...] = dv_sum[...].reshape(n, page, HD).astype(jnp.bfloat16)

        @pl.loop(1, n)
        def _(step):
            d = lax.rem(me + step, n)
            pack_back(h, d)
            pltpu.make_async_remote_copy(
                src_ref=back.at[h, d],
                dst_ref=home.at[h, me],
                send_sem=back_sem.at[h],
                recv_sem=home_sem.at[h],
                device_id=(d // n_head, lax.rem(d, n_head)),
                device_id_type=MESH,
            ).start()

        pack_back(h, me)
        pltpu.make_async_copy(back.at[h, me], home.at[h, me], own_sem.at[h]).start()

    @pl.loop(0, heads)
    def _(h):
        wait_all(home, h, home_sem)
        pltpu.make_async_copy(back.at[h, me], home.at[h, me], own_sem.at[h]).wait()
        wait_all(send, h, send_sem)
        wait_all(back, h, back_sem)


def deliver(heads, page, mine, home, q_out, k_out, v_out):
    for p in range(mine.shape[0]):
        bucket = mine[p]
        for g in range(home.shape[2]):
            for h in range(heads):
                column = (g * heads + h) * HD
                for a, dst in enumerate((q_out, k_out, v_out)):
                    dst[p, :, pl.ds(column, HD)] = home[h, bucket, g, pl.ds(a * page, page), :]


def shards(queries, keys, values, grad_out, page_dest, doc_start):
    n_bucket = lax.axis_size("bucket")
    n_head = lax.axis_size("head")
    n = n_bucket * n_head
    tok_dev, width = queries.shape
    page = tok_dev // n_bucket
    heads = width // n_head // HD
    seg = n * page
    block_slots = 2 * n_bucket
    block = block_slots * page
    mine, table = routing(
        page_dest, doc_start, lax.axis_index("bucket"), lax.axis_index("head"),
        n_bucket, n_head, block_slots,
    )
    low = jnp.bfloat16
    back_rows = -(-3 * page // 16) * 16
    smem = pl.BlockSpec(memory_space=pltpu.SMEM)
    hbm = pl.BlockSpec(memory_space=pl.ANY)
    pairs = heads * seg * seg // 2
    home = pl.pallas_call(
        functools.partial(kernel, n_bucket, n_head, heads, page, block),
        out_shape=jax.ShapeDtypeStruct((heads, n, back_rows, HD), low),
        in_specs=[smem] + [hbm] * 4,
        out_specs=hbm,
        scratch_shapes=[
            pltpu.VMEM((n_bucket, page, width), low),
            pltpu.VMEM((n_bucket, page, width), low),
            pltpu.VMEM((n_bucket, page, width), low),
            pltpu.VMEM((n_bucket, page, width), low),
            pltpu.VMEM((heads, n, 4 * page, HD), low),
            pltpu.VMEM((heads, n, 4 * page, HD), low),
            pltpu.VMEM((heads, n, back_rows, HD), low),
            pltpu.VMEM((n, 4 * page, HD), low),
            pltpu.VMEM((seg, HD), low),
            pltpu.VMEM((seg, HD), low),
            pltpu.VMEM((seg, HD), low),
            pltpu.VMEM((seg, HD), low),
            pltpu.VMEM((HD, seg), low),
            pltpu.VMEM((n, page, HD), low),
            pltpu.VMEM((n, page, HD), low),
            pltpu.VMEM((n, page, HD), low),
            pltpu.VMEM((seg, HD), jnp.float32),
            pltpu.VMEM((seg, HD), jnp.float32),
            pltpu.SemaphoreType.DMA((heads,)),
            pltpu.SemaphoreType.DMA((heads,)),
            pltpu.SemaphoreType.DMA((heads,)),
            pltpu.SemaphoreType.DMA((heads,)),
            pltpu.SemaphoreType.DMA((heads,)),
            pltpu.SemaphoreType.DMA((4,)),
        ],
        compiler_params=pltpu.CompilerParams(
            collective_id=0, has_side_effects=True, vmem_limit_bytes=56 * 1024 * 1024
        ),
        cost_estimate=pl.CostEstimate(
            flops=10 * pairs * HD, bytes_accessed=14 * tok_dev * width, transcendentals=pairs
        ),
    )(table, *(a.reshape(n_bucket, page, width) for a in (queries, keys, values, grad_out)))
    groups = max(1, n_head // 4)
    outs = pl.pallas_call(
        functools.partial(deliver, heads, page),
        grid=(n_head // groups,),
        out_shape=[jax.ShapeDtypeStruct((n_bucket, page, width), low)] * 3,
        in_specs=[
            smem,
            pl.BlockSpec((heads, n_bucket, groups, back_rows, HD), lambda g: (0, 0, g, 0, 0)),
        ],
        out_specs=[pl.BlockSpec((n_bucket, page, groups * heads * HD), lambda g: (0, 0, g))] * 3,
    )(mine, home.reshape(heads, n_bucket, n_head, back_rows, HD))
    return tuple(a.reshape(tok_dev, width) for a in outs)


def solution(mesh):
    split = P(("bucket", "head"), None)
    return jax.shard_map(
        shards,
        mesh=mesh,
        in_specs=(split, split, split, split, P(), P()),
        out_specs=(split, split, split),
        check_vma=False,
    )
```

```python
import functools

import jax
import jax.numpy as jnp
from jax import lax
from jax.experimental import pallas as pl
from jax.experimental.pallas import tpu as pltpu
from jax.sharding import PartitionSpec as P

HD = 128
LOG2E = 1.4426950408889634
MESH = pl.DeviceIdType.MESH


def routing(page_dest, doc_start, bucket_index, head_index, n_bucket, n_head, block_slots):
    slots = n_bucket * n_head
    dest = page_dest.reshape(slots, n_bucket)
    dest_bucket = dest // slots
    arrival_slot = jnp.sum(jnp.where(dest_bucket == bucket_index, dest % slots, 0), axis=1)
    slot_range = jnp.arange(slots, dtype=jnp.int32)
    slot_order = jnp.sum(
        jnp.where(arrival_slot[:, None] == slot_range[None, :], slot_range[:, None], 0), axis=0
    )
    mine = lax.dynamic_index_in_dim(
        dest_bucket, bucket_index * n_head + head_index, 0, keepdims=False
    )
    page_range = jnp.arange(n_bucket, dtype=jnp.int32)
    pick = jnp.sum(jnp.where(mine[:, None] == page_range[None, :], page_range[:, None], 0), axis=0)
    starts = lax.dynamic_slice_in_dim(doc_start, bucket_index * slots, slots)
    starts = starts.reshape(slots // block_slots, block_slots)[:, 0]
    firsts = jnp.arange(slots // block_slots, dtype=jnp.int32) * block_slots
    hidden = (firsts[None, :] < starts[:, None]).astype(jnp.int32)
    return mine, jnp.concatenate([pick, arrival_slot, slot_order, hidden.reshape(-1)])


def dot_nt(a, b):
    return lax.dot_general(a, b, (((1,), (1,)), ((), ())), preferred_element_type=jnp.float32)


def dot(a, b):
    return jnp.dot(a, b, preferred_element_type=jnp.float32)


def kernel(
    n_bucket, n_head, heads, page, block,
    table,
    q_hbm, k_hbm, v_hbm, g_hbm,
    home,
    q_in, k_in, v_in, g_in,
    send, recv, back, stage,
    q_s, k_s, v_s, g_s, k_t, dq, dk, dv, dk_sum, dv_sum,
    send_sem, recv_sem, back_sem, home_sem, own_sem, load_sem,
):
    n = n_bucket * n_head
    me = lax.axis_index("bucket") * n_head + lax.axis_index("head")
    seg = n * page
    blocks = seg // block
    scale = float(HD) ** (-0.5)

    arrival_at = n_bucket
    order_at = arrival_at + n
    hidden_at = order_at + n

    loads = [
        pltpu.make_async_copy(src, dst, load_sem.at[a])
        for a, (src, dst) in enumerate(
            ((q_hbm, q_in), (k_hbm, k_in), (v_hbm, v_in), (g_hbm, g_in))
        )
    ]
    for load in loads:
        load.start()

    barrier = pltpu.get_barrier_semaphore()

    @pl.loop(1, n)
    def _(step):
        d = lax.rem(me + step, n)
        pl.semaphore_signal(
            barrier, inc=1, device_id=(d // n_head, lax.rem(d, n_head)), device_id_type=MESH
        )

    halves = 2 if n_head % 2 == 0 else 1

    def target(step):
        pair = step // halves
        ahead = lax.rem(step, halves) * (n_head // halves) + pair // n_bucket
        b = lax.rem(lax.axis_index("bucket") + lax.rem(pair, n_bucket), n_bucket)
        return b * n_head + lax.rem(lax.axis_index("head") + ahead, n_head)

    def pack(h, d, where):
        from_page = table[d // n_head]
        column = pl.multiple_of((lax.rem(d, n_head) * heads + h) * HD, HD)
        for a, src in enumerate((q_in, k_in, v_in, g_in)):
            where[h, d, pl.ds(a * page, page), :] = src[from_page, :, pl.ds(column, HD)]

    pl.semaphore_wait(barrier, n - 1)
    for load in loads:
        load.wait()

    @pl.loop(0, heads)
    def _(h):
        @pl.loop(1, n)
        def _(step):
            d = target(step)
            pack(h, d, send)
            pltpu.make_async_remote_copy(
                src_ref=send.at[h, d],
                dst_ref=recv.at[h, me],
                send_sem=send_sem.at[h],
                recv_sem=recv_sem.at[h],
                device_id=(d // n_head, lax.rem(d, n_head)),
                device_id_type=MESH,
            ).start()

        pack(h, me, recv)

    key_row = lax.broadcasted_iota(jnp.int32, (block, block), 0)
    query_col = lax.broadcasted_iota(jnp.int32, (block, block), 1)
    causal = key_row <= query_col

    def attend(i):
        rows = (i + 1) * block
        here = pl.ds(i * block, block)
        q_b = q_s[here, :]
        g_b = g_s[here, :]
        s = dot_nt(k_s[pl.ds(0, rows), :], q_b)
        parts = []
        for j in range(i):
            lower = table[hidden_at + i * blocks + j].astype(jnp.float32) * -3e38
            parts.append(s[j * block : (j + 1) * block] + lower)
        parts.append(jnp.where(causal, s[i * block :], -jnp.inf))
        s = jnp.concatenate(parts, axis=0) if i else parts[0]
        top = jnp.max(s, axis=0, keepdims=True)
        w = jnp.exp2((s - top) * (scale * LOG2E))
        p = (w * (1.0 / jnp.sum(w, axis=0, keepdims=True))).astype(jnp.bfloat16)
        gp = dot_nt(v_s[pl.ds(0, rows), :], g_b)
        p32 = p.astype(jnp.float32)
        row_dot = jnp.sum(p32 * gp, axis=0, keepdims=True)
        gs = (p32 * ((gp - row_dot) * scale)).astype(jnp.bfloat16)
        if i == blocks - 1:
            dv_sum[...] = dot(p, g_b)
            dk_sum[...] = dot(gs, q_b)
        else:
            dv_sum[pl.ds(0, rows), :] += dot(p, g_b)
            dk_sum[pl.ds(0, rows), :] += dot(gs, q_b)
        gq = dot(k_t[:, pl.ds(0, rows)], gs).T.reshape(block // page, page, HD)
        dq[pl.ds(i * (block // page), block // page)] = gq.astype(jnp.bfloat16)

    def wait_all(ref, h, sem):
        part = ref.at[h, pl.ds(0, n - 1)]
        pltpu.make_async_copy(part, part, sem.at[h]).wait()

    def pack_back(h, d):
        slot = table[arrival_at + d]
        for a, src in enumerate((dq, dk, dv)):
            back[h, d, pl.ds(a * page, page), :] = src[slot]

    @pl.loop(0, heads)
    def _(h):
        wait_all(recv, h, recv_sem)

        @pl.loop(0, n)
        def _(s):
            stage[s] = recv[h, s]

        @pl.loop(0, n)
        def _(s):
            src = table[order_at + s]
            to = pl.ds(pl.multiple_of(s * page, page), page)
            for a, dst in enumerate((q_s, k_s, v_s, g_s)):
                dst[to, :] = stage[src, pl.ds(a * page, page), :]

        k_t[...] = k_s[...].T
        for i in reversed(range(blocks)):
            attend(i)
        dk[...] = dk_sum[...].reshape(n, page, HD).astype(jnp.bfloat16)
        dv[...] = dv_sum[...].reshape(n, page, HD).astype(jnp.bfloat16)

        @pl.loop(1, n)
        def _(step):
            d = target(step)
            pack_back(h, d)
            pltpu.make_async_remote_copy(
                src_ref=back.at[h, d],
                dst_ref=home.at[h, me],
                send_sem=back_sem.at[h],
                recv_sem=home_sem.at[h],
                device_id=(d // n_head, lax.rem(d, n_head)),
                device_id_type=MESH,
            ).start()

        pack_back(h, me)
        pltpu.make_async_copy(back.at[h, me], home.at[h, me], own_sem.at[h]).start()

    @pl.loop(0, heads)
    def _(h):
        wait_all(home, h, home_sem)
        pltpu.make_async_copy(back.at[h, me], home.at[h, me], own_sem.at[h]).wait()
        wait_all(send, h, send_sem)
        wait_all(back, h, back_sem)


def deliver(heads, page, mine, home, q_out, k_out, v_out):
    for p in range(mine.shape[0]):
        bucket = mine[p]
        for g in range(home.shape[2]):
            for h in range(heads):
                column = (g * heads + h) * HD
                for a, dst in enumerate((q_out, k_out, v_out)):
                    dst[p, :, pl.ds(column, HD)] = home[h, bucket, g, pl.ds(a * page, page), :]


def shards(queries, keys, values, grad_out, page_dest, doc_start):
    n_bucket = lax.axis_size("bucket")
    n_head = lax.axis_size("head")
    n = n_bucket * n_head
    tok_dev, width = queries.shape
    page = tok_dev // n_bucket
    heads = width // n_head // HD
    seg = n * page
    block_slots = 2 * n_bucket
    block = block_slots * page
    mine, table = routing(
        page_dest, doc_start, lax.axis_index("bucket"), lax.axis_index("head"),
        n_bucket, n_head, block_slots,
    )
    low = jnp.bfloat16
    back_rows = -(-3 * page // 16) * 16
    smem = pl.BlockSpec(memory_space=pltpu.SMEM)
    hbm = pl.BlockSpec(memory_space=pl.ANY)
    pairs = heads * seg * seg // 2
    home = pl.pallas_call(
        functools.partial(kernel, n_bucket, n_head, heads, page, block),
        out_shape=jax.ShapeDtypeStruct((heads, n, back_rows, HD), low),
        in_specs=[smem] + [hbm] * 4,
        out_specs=hbm,
        scratch_shapes=[
            pltpu.VMEM((n_bucket, page, width), low),
            pltpu.VMEM((n_bucket, page, width), low),
            pltpu.VMEM((n_bucket, page, width), low),
            pltpu.VMEM((n_bucket, page, width), low),
            pltpu.VMEM((heads, n, 4 * page, HD), low),
            pltpu.VMEM((heads, n, 4 * page, HD), low),
            pltpu.VMEM((heads, n, back_rows, HD), low),
            pltpu.VMEM((n, 4 * page, HD), low),
            pltpu.VMEM((seg, HD), low),
            pltpu.VMEM((seg, HD), low),
            pltpu.VMEM((seg, HD), low),
            pltpu.VMEM((seg, HD), low),
            pltpu.VMEM((HD, seg), low),
            pltpu.VMEM((n, page, HD), low),
            pltpu.VMEM((n, page, HD), low),
            pltpu.VMEM((n, page, HD), low),
            pltpu.VMEM((seg, HD), jnp.float32),
            pltpu.VMEM((seg, HD), jnp.float32),
            pltpu.SemaphoreType.DMA((heads,)),
            pltpu.SemaphoreType.DMA((heads,)),
            pltpu.SemaphoreType.DMA((heads,)),
            pltpu.SemaphoreType.DMA((heads,)),
            pltpu.SemaphoreType.DMA((heads,)),
            pltpu.SemaphoreType.DMA((4,)),
        ],
        compiler_params=pltpu.CompilerParams(
            collective_id=0, has_side_effects=True, vmem_limit_bytes=56 * 1024 * 1024
        ),
        cost_estimate=pl.CostEstimate(
            flops=10 * pairs * HD, bytes_accessed=14 * tok_dev * width, transcendentals=pairs
        ),
    )(table, *(a.reshape(n_bucket, page, width) for a in (queries, keys, values, grad_out)))
    groups = max(1, n_head // 4)
    outs = pl.pallas_call(
        functools.partial(deliver, heads, page),
        grid=(n_head // groups,),
        out_shape=[jax.ShapeDtypeStruct((n_bucket, page, width), low)] * 3,
        in_specs=[
            smem,
            pl.BlockSpec((heads, n_bucket, groups, back_rows, HD), lambda g: (0, 0, g, 0, 0)),
        ],
        out_specs=[pl.BlockSpec((n_bucket, page, groups * heads * HD), lambda g: (0, 0, g))] * 3,
    )(mine, home.reshape(heads, n_bucket, n_head, back_rows, HD))
    return tuple(a.reshape(tok_dev, width) for a in outs)


def solution(mesh):
    split = P(("bucket", "head"), None)
    return jax.shard_map(
        shards,
        mesh=mesh,
        in_specs=(split, split, split, split, P(), P()),
        out_specs=(split, split, split),
        check_vma=False,
    )
```
